512 devices in a mesh: dp: 32 (over z, core), tensor: 16 (over y, x).
Axes of the slice: x: 4, y: 4, z: 16, core: 2. Of those that a mesh axis runs over, the one named last changes fastest.
Arguments:
- grads: bfloat16 [32, 2048, 5632], P('dp', None, 'tensor'), may hold values from -6 to 6
- errors: bfloat16 [32, 2048, 5632], P('dp', None, 'tensor'), may hold values from -4 to 4
- q_start: float32 [5632, 32], P('tensor'), may hold values from -6 to 6
Outputs:
- new_errors: bfloat16 [32, 2048, 5632], P('dp', None, 'tensor')
- p_hat: float32 [2048, 32], replicated
- q_new: float32 [5632, 32], P('tensor')
The draws below stay inside these ranges and needn't reach their ends.
All inputs are finite; a program needn't handle non-finite values.
Results may differ from the reference program's by a relative error of at most 0.012.
Values sent between devices are 32-bit elements; how exact they have to be, the bound alone decides.
A program may use at most 64 MiB of HBM per device.

```python
import jax
import jax.numpy as jnp
from jax import lax

D = 2048
F = 5632
RANK = 32
N_DP = 32


def shard_levels(stream_key, shape, cuts, least, top_value):
    loudness = 1.0
    for axis_at, shards_of in cuts:
        heights = jax.random.uniform(jax.random.fold_in(jax.random.fold_in(stream_key, 6), axis_at), (shards_of,), jnp.float32, least / len(cuts), top_value / len(cuts))
        loudness = loudness * jnp.repeat(jnp.exp(heights), shape[axis_at] // shards_of).reshape((-1,) + (1,) * (len(shape) - 1 - axis_at))
    return loudness


def gaussian(rng, shape, spread, reach, pieces=(), kind=jnp.bfloat16):
    drawn = spread * jax.random.normal(rng, shape, jnp.float32)
    if pieces:
        drawn = drawn * shard_levels(rng, shape, pieces, -0.22, 0.18)
    return jnp.clip(drawn, -reach, reach).astype(kind)


def setup_inputs(seed: int = 0) -> dict:
    keys = jax.random.split(jax.random.key(seed), 4)
    grads = gaussian(keys[0], (N_DP, D, F), 1.0, 6.0, ((0, 32), (2, 16)))
    errors = gaussian(keys[1], (N_DP, D, F), 0.5, 4.0, ((0, 32), (2, 16)))
    q_start = gaussian(keys[2], (F, RANK), 1.0, 6.0, ((0, 16),), jnp.float32)
    return dict(grads=grads, errors=errors, q_start=q_start)


def orthogonal(p_sum):
    gram_matrix = jnp.dot(p_sum.T, p_sum, precision=lax.Precision.HIGHEST)
    lower_factor = jnp.linalg.cholesky(gram_matrix)
    return lax.linalg.triangular_solve(lower_factor, p_sum, left_side=False, lower=True, transpose_a=True)

def reference(grads, errors, q_start):
    q_narrow = q_start.astype(jnp.bfloat16)

    def merge_one(grad_one, error_one):
        return (grad_one.astype(jnp.float32) + error_one.astype(jnp.float32)).astype(jnp.bfloat16)

    def add_left(total, pair):
        merged = merge_one(pair[0], pair[1])
        return (total + jnp.dot(merged.astype(jnp.float32), q_narrow.astype(jnp.float32), preferred_element_type=jnp.float32), None)
    p_sum, _ = lax.scan(add_left, jnp.zeros((D, RANK), jnp.float32), (grads, errors))
    p_hat = orthogonal(p_sum)
    p_narrow = p_hat.astype(jnp.bfloat16)

    def add_right(total, pair):
        merged = merge_one(pair[0], pair[1])
        term = lax.dot_general(merged.astype(jnp.float32), p_narrow.astype(jnp.float32), (((0,), (0,)), ((), ())), preferred_element_type=jnp.float32)
        return (total + term, None)
    q_sum, _ = lax.scan(add_right, jnp.zeros((F, RANK), jnp.float32), (grads, errors))
    q_new = q_sum / N_DP
    delta = jnp.dot(p_hat, q_new.T, precision=lax.Precision.HIGHEST)

    def update(pair):
        merged = merge_one(pair[0], pair[1])
        return (merged.astype(jnp.float32) - delta).astype(jnp.bfloat16)
    new_errors = lax.map(update, (grads, errors))
    return (new_errors, p_hat, q_new)
```

```python
import functools

import jax
import jax.numpy as jnp
from jax import lax
from jax.experimental import pallas as pl
from jax.experimental.pallas import tpu as pltpu
from jax.sharding import PartitionSpec as P

MESH = pl.DeviceIdType.MESH
HIGHEST = lax.Precision.HIGHEST
F32, BF16 = jnp.float32, jnp.bfloat16

RANK = 32
ROWS = 2048
COLS = 352
WIDE = 384
STEP = 256
STEPS = ROWS // STEP

FAR = {0: 0, 1: 1, 2: 2, 3: 1}
OFFSETS = sorted(
    ((j, y, x) for j in range(2) for y in range(4) for x in range(4) if (j, y, x) != (0, 0, 0)),
    key=lambda o: -(o[0] + FAR[o[1]] + FAR[o[2]]),
)
GROUPS = [4, 3, 5, 2, 6, 1, 7]


def split3(value):
    hi = value.astype(BF16)
    rest = value - hi.astype(F32)
    mid = rest.astype(BF16)
    lo = (rest - mid.astype(F32)).astype(BF16)
    return hi, mid, lo


def kernel(
    grads, errors, q_start, merged_out, p_split, p_out, q_out,
    q_in, gbuf, ebuf, parts_buf, pt, core_rx, a_src, a_rx, b_src, b_rx, p_full,
    q_part, d_rx, e_src, e_rx, q_full,
    q_sem, load_sem, core_send, core_recv, a_send, a_recv, b_send, b_recv, c_send, c_recv,
    f_send, f_recv, d_send, d_recv, e_send, e_recv, g_send, g_recv,
):
    dp, tensor = lax.axis_index("dp"), lax.axis_index("tensor")
    z, core = dp // 2, dp % 2
    group, bit = z // 2, z % 2
    member = (bit + group // 4) % 2
    y, x = tensor // 4, tensor % 4

    def chip(a, j):
        return 2 * a + (j + a // 4) % 2

    def plane_peer(o):
        j, py, px = (member + o[0]) % 2, (y + o[1]) % 4, (x + o[2]) % 4
        t = py * 4 + px
        return (chip(group, j) * 2 + core, t), j * 16 + t

    def group_peer(k):
        a = (group + k) % 8
        return (chip(a, member) * 2 + core, tensor)

    sibling = (z * 2 + 1 - core, tensor)
    across = (chip(group, 1 - member) * 2 + 1 - core, tensor)
    beside = (chip(group, 1 - member) * 2 + core, tensor)
    mine = member * 16 + tensor

    def cols(i):
        return pl.ds(pl.multiple_of(i * STEP, STEP), STEP)

    def load(i):
        at = ((1 - core) * (STEPS // 2) + i) % STEPS
        return (
            pltpu.make_async_copy(grads.at[:, cols(at)], gbuf.at[:, cols(at)], load_sem.at[0, i]),
            pltpu.make_async_copy(errors.at[:, cols(at)], ebuf.at[:, cols(at)], load_sem.at[1, i]),
        )

    q_copy = pltpu.make_async_copy(q_start, q_in, q_sem)
    q_copy.start()
    for i in range(STEPS):
        for copy in load(i):
            copy.start()

    barrier = pltpu.get_barrier_semaphore()
    for k in GROUPS:
        pl.semaphore_signal(barrier, inc=1, device_id=group_peer(k), device_id_type=MESH)
    for o in OFFSETS:
        pl.semaphore_signal(barrier, inc=1, device_id=plane_peer(o)[0], device_id_type=MESH)
    pl.semaphore_signal(barrier, inc=1, device_id=across, device_id_type=MESH)
    pl.semaphore_signal(barrier, inc=1, device_id=sibling, device_id_type=MESH)

    q_copy.wait()
    q_narrow = q_in[...].astype(BF16)

    def left(i):
        for copy in load(i):
            copy.wait()
        at = ((1 - core) * (STEPS // 2) + i) % STEPS
        merged = (gbuf[:, cols(at)].astype(F32) + ebuf[:, cols(at)].astype(F32)).astype(BF16)
        merged_out[:, cols(at)] = merged
        part = jnp.dot(q_narrow, merged, preferred_element_type=F32)
        for h in range(2):
            pt[pl.ds(at * 8 + h * 4, 4)] = part[:, h * 128 : (h + 1) * 128].reshape(4, 8, 128)

    for i in range(STEPS // 2):
        left(i)
    pl.semaphore_wait(barrier, len(GROUPS) + len(OFFSETS) + 2)
    core_copy = pltpu.make_async_remote_copy(
        src_ref=pt.at[pl.ds((1 - core) * 32, 32)], dst_ref=core_rx,
        send_sem=core_send, recv_sem=core_recv, device_id=sibling, device_id_type=MESH,
    )
    core_copy.start()
    for i in range(STEPS // 2, STEPS):
        left(i)
    core_copy.wait_recv()
    a_src[...] = pt[pl.ds(core * 32, 32)] + core_rx[...]

    for n, o in enumerate(OFFSETS):
        device, chunk = plane_peer(o)
        pltpu.make_async_remote_copy(
            src_ref=a_src.at[chunk], dst_ref=a_rx.at[n],
            send_sem=a_send, recv_sem=a_recv, device_id=device, device_id_type=MESH,
        ).start()

    def all_of(ref, send, recv):
        return pltpu.make_async_remote_copy(
            src_ref=ref, dst_ref=ref, send_sem=send, recv_sem=recv, device_id=sibling, device_id_type=MESH
        )

    all_a = all_of(a_rx, a_send, a_recv)
    all_a.wait_recv()
    total = a_src[mine]
    for n in range(len(OFFSETS)):
        total = total + a_rx[n]
    b_src[...] = total
    b_rx[group] = total

    for k in GROUPS:
        pltpu.make_async_remote_copy(
            src_ref=b_src, dst_ref=b_rx.at[group],
            send_sem=b_send, recv_sem=b_recv, device_id=group_peer(k), device_id_type=MESH,
        ).start()
    all_b = all_of(b_rx.at[pl.ds(0, 7)], b_send, b_recv)
    all_b.wait_recv()
    total = b_rx[0]
    for k in range(1, 8):
        total = total + b_rx[k]
    p_full[core * 32 + mine] = total

    for n, o in enumerate(OFFSETS):
        pltpu.make_async_remote_copy(
            src_ref=p_full.at[core * 32 + mine], dst_ref=p_full.at[core * 32 + mine],
            send_sem=c_send, recv_sem=c_recv, device_id=plane_peer(o)[0], device_id_type=MESH,
        ).start()
    all_c = all_of(p_full.at[pl.ds(0, 31)], c_send, c_recv)
    all_c.wait_recv()
    half = pl.ds(core * 32, 32)
    half_copy = pltpu.make_async_remote_copy(
        src_ref=p_full.at[half], dst_ref=p_full.at[half],
        send_sem=f_send, recv_sem=f_recv, device_id=sibling, device_id_type=MESH,
    )
    half_copy.start()

    def right(at):
        tiles = [p_full[pl.ds(at * 8 + h * 4, 4)].reshape(RANK, 128) for h in range(2)]
        parts = jnp.concatenate(split3(jnp.concatenate(tiles, axis=1)), axis=0)
        parts_buf[:, cols(at)] = parts
        return lax.dot_general(
            parts, merged_out[:, cols(at)], (((1,), (1,)), ((), ())), preferred_element_type=F32
        )

    def right_half(c):
        acc = right(c * (STEPS // 2))
        for i in range(1, STEPS // 2):
            acc = acc + right(c * (STEPS // 2) + i)
        return acc

    acc = right_half(core)
    half_copy.wait_recv()
    acc = acc + right_half(1 - core)
    acc = acc[2 * RANK :] + acc[RANK : 2 * RANK] + acc[0:RANK]
    q_part[:, :, 0:COLS] = acc.reshape(4, 8, COLS)
    q_part[:, :, COLS:] = jnp.zeros((4, 8, WIDE - COLS), F32)

    def owner(j, c):
        return j * 2 + c

    me = owner(member, core)
    partners = (
        (across, owner(1 - member, 1 - core)),
        (beside, owner(1 - member, core)),
        (sibling, owner(member, 1 - core)),
    )
    for n, (device, chunk) in enumerate(partners):
        pltpu.make_async_remote_copy(
            src_ref=q_part.at[chunk], dst_ref=d_rx.at[n],
            send_sem=d_send, recv_sem=d_recv, device_id=device, device_id_type=MESH,
        ).start()
    gram = lax.dot_general(
        parts_buf[...], parts_buf[...], (((1,), (1,)), ((), ())), preferred_element_type=F32
    )
    gram = gram[2 * RANK :] + gram[RANK : 2 * RANK] + gram[0:RANK]
    gram = gram[:, 2 * RANK :] + gram[:, RANK : 2 * RANK] + gram[:, 0:RANK]
    all_d = all_of(d_rx, d_send, d_recv)
    all_d.wait_recv()
    total = q_part[me] + d_rx[0] + d_rx[1] + d_rx[2]
    e_src[...] = total
    e_rx[group] = total
    for k in GROUPS:
        pltpu.make_async_remote_copy(
            src_ref=e_src, dst_ref=e_rx.at[group],
            send_sem=e_send, recv_sem=e_recv, device_id=group_peer(k), device_id_type=MESH,
        ).start()

    row = lax.broadcasted_iota(jnp.int32, (RANK, 2 * RANK), 0)
    col = lax.broadcasted_iota(jnp.int32, (RANK, 2 * RANK), 1)
    unit = jnp.where(col == row + RANK, 1.0, 0.0).astype(F32)
    work = jnp.concatenate([gram, unit[:, RANK:]], axis=1)
    below = lax.broadcasted_iota(jnp.int32, (RANK, 1), 0)
    for k in range(RANK - 1):
        pivot = work[k : k + 1, :]
        factor = work[:, k : k + 1] / work[k : k + 1, k : k + 1]
        work = work - jnp.where(below > k, factor, 0.0) * pivot
    diagonal = jnp.sum(jnp.where(row == col, work, 0.0), axis=1, keepdims=True)
    inverse = work[:, RANK:] / jnp.sqrt(diagonal)

    for i in range(STEPS):
        tiles = [p_full[pl.ds(i * 8 + h * 4, 4)].reshape(RANK, 128) for h in range(2)]
        p_hat = jnp.dot(inverse, jnp.concatenate(tiles, axis=1), precision=HIGHEST, preferred_element_type=F32)
        p_out[:, cols(i)] = p_hat
        hi, mid, lo = split3(p_hat)
        p_split[:, cols(i)] = jnp.concatenate([hi, mid, hi, mid, lo, hi], axis=0)

    all_e = all_of(e_rx.at[pl.ds(0, 7)], e_send, e_recv)
    all_e.wait_recv()
    total = e_rx[0]
    for k in range(1, 8):
        total = total + e_rx[k]
    q_full[me] = total
    for n, (device, _) in enumerate(partners):
        pltpu.make_async_remote_copy(
            src_ref=q_full.at[me], dst_ref=q_full.at[me],
            send_sem=g_send, recv_sem=g_recv, device_id=device, device_id_type=MESH,
        ).start()
    all_g = all_of(q_full.at[pl.ds(0, 3)], g_send, g_recv)
    all_g.wait_recv()
    q_sum = q_full[...].reshape(RANK, WIDE)
    q_new = jnp.dot(inverse, q_sum, precision=HIGHEST, preferred_element_type=F32) * (1.0 / 32.0)
    q_out[...] = q_new[:, 0:COLS]
    core_copy.wait_send()
    all_a.wait_send()
    all_b.wait_send()
    all_c.wait_send()
    half_copy.wait_send()
    all_d.wait_send()
    all_e.wait_send()
    all_g.wait_send()


def update_kernel(merged, p_split, p_hat, q_new, new_errors, p_out, q_out, stage, out_sem, side_sem):
    p_copy = pltpu.make_async_copy(p_hat, p_out, side_sem.at[0])
    q_copy = pltpu.make_async_copy(q_new, q_out, side_sem.at[1])
    p_copy.start()
    q_copy.start()
    hi, mid, lo = split3(q_new[...].T)
    q_split = jnp.concatenate([hi, hi, mid, mid, hi, lo], axis=1)

    def store(i):
        at = pl.ds(i * STEP, STEP)
        return pltpu.make_async_copy(stage.at[:, at], new_errors.at[:, at], out_sem.at[i])

    for i in range(STEPS):
        at = pl.ds(i * STEP, STEP)
        delta = jnp.dot(q_split, p_split[:, at], preferred_element_type=F32)
        stage[:, at] = (merged[:, at].astype(F32) - delta).astype(BF16)
        store(i).start()
    p_copy.wait()
    q_copy.wait()
    for i in range(STEPS):
        store(i).wait()


def body(grads, errors, q_start):
    hbm_spec = pl.BlockSpec(memory_space=pltpu.HBM)
    vmem_spec = pl.BlockSpec(memory_space=pltpu.VMEM)
    dma = pltpu.SemaphoreType.DMA
    tile = (8, 128)
    strip = (8, WIDE)
    merged, p_split, p_hat, q_new = pl.pallas_call(
        kernel,
        name="factors",
        out_shape=(
            jax.ShapeDtypeStruct((COLS, ROWS), BF16),
            jax.ShapeDtypeStruct((6 * RANK, ROWS), BF16),
            jax.ShapeDtypeStruct((RANK, ROWS), F32),
            jax.ShapeDtypeStruct((RANK, COLS), F32),
        ),
        in_specs=[hbm_spec, hbm_spec, hbm_spec],
        out_specs=(vmem_spec,) * 4,
        scratch_shapes=[
            pltpu.VMEM((RANK, COLS), F32),
            pltpu.VMEM((COLS, ROWS), BF16),
            pltpu.VMEM((COLS, ROWS), BF16),
            pltpu.VMEM((3 * RANK, ROWS), BF16),
            pltpu.VMEM((64,) + tile, F32),
            pltpu.VMEM((32,) + tile, F32),
            pltpu.VMEM((32,) + tile, F32),
            pltpu.VMEM((31,) + tile, F32),
            pltpu.VMEM(tile, F32),
            pltpu.VMEM((8,) + tile, F32),
            pltpu.VMEM((64,) + tile, F32),
            pltpu.VMEM((4,) + strip, F32),
            pltpu.VMEM((3,) + strip, F32),
            pltpu.VMEM(strip, F32),
            pltpu.VMEM((8,) + strip, F32),
            pltpu.VMEM((4,) + strip, F32),
            dma,
            dma((2, STEPS)),
        ]
        + [dma] * 16,
        compiler_params=pltpu.CompilerParams(
            collective_id=0, has_side_effects=True, vmem_limit_bytes=32 * 1024 * 1024
        ),
    )(*(pltpu.with_memory_space_constraint(a, pltpu.HBM) for a in (grads[0].T, errors[0].T, q_start.T)))
    new_errors, p_hat, q_new = pl.pallas_call(
        update_kernel,
        name="update",
        out_shape=(
            jax.ShapeDtypeStruct((COLS, ROWS), BF16),
            jax.ShapeDtypeStruct((RANK, ROWS), F32),
            jax.ShapeDtypeStruct((RANK, COLS), F32),
        ),
        in_specs=[vmem_spec] * 4,
        out_specs=(hbm_spec,) * 3,
        scratch_shapes=[pltpu.VMEM((COLS, ROWS), BF16), dma((STEPS,)), dma((2,))],
        compiler_params=pltpu.CompilerParams(vmem_limit_bytes=16 * 1024 * 1024),
    )(merged, p_split, p_hat, q_new)
    return new_errors.T[None], p_hat.T, q_new.T


def solution(mesh):
    placed = (P("dp", None, "tensor"), P("dp", None, "tensor"), P("tensor", None))
    return jax.shard_map(
        body,
        mesh=mesh,
        in_specs=placed,
        out_specs=(P("dp", None, "tensor"), P(), P("tensor", None)),
        check_vma=False,
    )
```

```python
import functools

import jax
import jax.numpy as jnp
from jax import lax
from jax.experimental import pallas as pl
from jax.experimental.pallas import tpu as pltpu
from jax.sharding import PartitionSpec as P

MESH = pl.DeviceIdType.MESH
HIGHEST = lax.Precision.HIGHEST
F32, BF16 = jnp.float32, jnp.bfloat16

RANK = 32
ROWS = 2048
COLS = 352
WIDE = 384
STEP = 256
STEPS = ROWS // STEP

FAR = {0: 0, 1: 1, 2: 2, 3: 1}
OFFSETS = sorted(
    ((j, y, x) for j in range(2) for y in range(4) for x in range(4) if (j, y, x) != (0, 0, 0)),
    key=lambda o: -(o[0] + FAR[o[1]] + FAR[o[2]]),
)
GROUPS = [4, 3, 5, 2, 6, 1, 7]


def split3(value):
    hi = value.astype(BF16)
    rest = value - hi.astype(F32)
    mid = rest.astype(BF16)
    lo = (rest - mid.astype(F32)).astype(BF16)
    return hi, mid, lo


def kernel(
    grads, errors, q_start, merged_out, p_split, p_out, q_out,
    q_in, gbuf, ebuf, parts_buf, pt, core_rx, a_src, a_rx, b_src, b_rx, p_full,
    q_part, d_rx, e_src, e_rx, q_full, m_src, m_rx, m_hi, m_lo,
    ready, m_send, m_recv, q_sem, load_sem, core_send, core_recv, a_send, a_recv, b_send, b_recv, c_send, c_recv,
    f_send, f_recv, d_send, d_recv, e_send, e_recv, g_send, g_recv,
):
    dp, tensor = lax.axis_index("dp"), lax.axis_index("tensor")
    z, core = lax.div(dp, 2), lax.rem(dp, 2)
    group, bit = lax.div(z, 2), lax.rem(z, 2)
    member = lax.rem(bit + lax.div(group, 4), 2)
    y, x = lax.div(tensor, 4), lax.rem(tensor, 4)
    columns_of = [lax.rem(x + k, 4) for k in range(4)]
    rows_of = [lax.rem(y + k, 4) * 4 for k in range(4)]
    members = [member, 1 - member]
    in_pair = [dp, 4 * group + 2 * (1 - bit) + core]

    def plane_peer(o):
        t = rows_of[o[1]] + columns_of[o[2]]
        return (in_pair[o[0]], t), members[o[0]] * 16 + t

    def group_at(a):
        return (4 * a + 2 * (member if a < 4 else 1 - member) + core, tensor)

    def group_peer(k):
        a = lax.rem(group + k, 8)
        return (4 * a + 2 * lax.rem(member + lax.div(a, 4), 2) + core, tensor)

    other = 1 - core
    sibling = (dp + other - core, tensor)
    beside = (in_pair[1], tensor)
    across = (in_pair[1] + other - core, tensor)
    mine = member * 16 + tensor

    def cols(i):
        return pl.ds(pl.multiple_of(i * STEP, STEP), STEP)

    def half_at(i):
        return (other if i < STEPS // 2 else core) * (STEPS // 2) + i % (STEPS // 2)

    def load(i):
        at = half_at(i)
        return (
            pltpu.make_async_copy(grads.at[:, cols(at)], gbuf.at[:, cols(at)], load_sem.at[0, i]),
            pltpu.make_async_copy(errors.at[:, cols(at)], ebuf.at[:, cols(at)], load_sem.at[1, i]),
        )

    q_copy = pltpu.make_async_copy(q_start, q_in, q_sem)
    q_copy.start()
    for i in range(STEPS):
        for copy in load(i):
            copy.start()

    barrier = pltpu.get_barrier_semaphore()
    for a in range(8):

        @pl.when(group < a)
        def _():
            pl.semaphore_signal(barrier, inc=1, device_id=group_at(a), device_id_type=MESH)

    for o in OFFSETS:
        pl.semaphore_signal(barrier, inc=1, device_id=plane_peer(o)[0], device_id_type=MESH)
    pl.semaphore_signal(barrier, inc=1, device_id=across, device_id_type=MESH)
    pl.semaphore_signal(barrier, inc=1, device_id=sibling, device_id_type=MESH)

    q_copy.wait()
    q_narrow = q_in[...].astype(BF16)

    def left(i):
        for copy in load(i):
            copy.wait()
        at = half_at(i)
        merged = (gbuf[:, cols(at)].astype(F32) + ebuf[:, cols(at)].astype(F32)).astype(BF16)
        merged_out[:, cols(at)] = merged
        part = jnp.dot(q_narrow, merged, preferred_element_type=F32)
        for h in range(2):
            pt[pl.ds(at * 8 + h * 4, 4)] = part[:, h * 128 : (h + 1) * 128].reshape(4, 8, 128)

    for i in range(STEPS // 2):
        left(i)
    pl.semaphore_wait(barrier, len(OFFSETS) + 2 + group)
    for a in range(8):

        @pl.when(group > a)
        def _():
            pl.semaphore_signal(ready, inc=1, device_id=group_at(a), device_id_type=MESH)

    core_copy = pltpu.make_async_remote_copy(
        src_ref=pt.at[pl.ds(other * 32, 32)], dst_ref=core_rx,
        send_sem=core_send, recv_sem=core_recv, device_id=sibling, device_id_type=MESH,
    )
    core_copy.start()
    for i in range(STEPS // 2, STEPS):
        left(i)
    core_copy.wait_recv()
    a_src[...] = pt[pl.ds(core * 32, 32)] + core_rx[...]

    for n, o in enumerate(OFFSETS):
        device, chunk = plane_peer(o)
        pltpu.make_async_remote_copy(
            src_ref=a_src.at[chunk], dst_ref=a_rx.at[n],
            send_sem=a_send, recv_sem=a_recv, device_id=device, device_id_type=MESH,
        ).start()

    def swap(i):
        part = pl.ds(i * STEP, STEP)
        return pltpu.make_async_remote_copy(
            src_ref=m_src.at[:, part], dst_ref=m_rx.at[:, part],
            send_sem=m_send.at[i], recv_sem=m_recv.at[i], device_id=sibling, device_id_type=MESH,
        )

    for i in range(STEPS // 2):
        m_src[:, i * STEP : (i + 1) * STEP] = merged_out[:, cols(half_at(i))].astype(F32)
        swap(i).start()

    def all_of(ref, send, recv):
        return pltpu.make_async_remote_copy(
            src_ref=ref, dst_ref=ref, send_sem=send, recv_sem=recv, device_id=sibling, device_id_type=MESH
        )

    all_a = all_of(a_rx, a_send, a_recv)
    all_a.wait_recv()
    total = a_src[mine]
    for n in range(len(OFFSETS)):
        total = total + a_rx[n]
    b_src[...] = total
    b_rx[group] = total

    def spread(a):
        pltpu.make_async_remote_copy(
            src_ref=b_src, dst_ref=b_rx.at[group],
            send_sem=b_send, recv_sem=b_recv, device_id=group_at(a), device_id_type=MESH,
        ).start()

    for a in range(7):

        @pl.when(group > a)
        def _():
            spread(a)

    @pl.when(group < 7)
    def _():
        pl.semaphore_wait(ready, 7 - group)

    for a in range(7, 0, -1):

        @pl.when(group < a)
        def _():
            spread(a)

    for i in range(STEPS // 2):
        part = slice(i * STEP, (i + 1) * STEP)
        swap(i).wait_recv()
        both = merged_out[:, cols(core * (STEPS // 2) + i)].astype(F32) + m_rx[:, part]
        hi = both.astype(BF16)
        m_hi[:, part] = hi
        m_lo[:, part] = (both - hi.astype(F32)).astype(BF16)

    all_b = all_of(b_rx.at[pl.ds(0, 7)], b_send, b_recv)
    all_b.wait_recv()
    total = b_rx[0]
    for k in range(1, 8):
        total = total + b_rx[k]
    p_full[core * 32 + mine] = total

    for n, o in enumerate(OFFSETS):
        pltpu.make_async_remote_copy(
            src_ref=p_full.at[core * 32 + mine], dst_ref=p_full.at[core * 32 + mine],
            send_sem=c_send, recv_sem=c_recv, device_id=plane_peer(o)[0], device_id_type=MESH,
        ).start()
    all_c = all_of(p_full.at[pl.ds(0, 31)], c_send, c_recv)
    all_c.wait_recv()
    half = pl.ds(core * 32, 32)
    half_copy = pltpu.make_async_remote_copy(
        src_ref=p_full.at[half], dst_ref=p_full.at[half],
        send_sem=f_send, recv_sem=f_recv, device_id=sibling, device_id_type=MESH,
    )
    half_copy.start()

    def left_parts(at):
        tiles = [p_full[pl.ds(at * 8 + h * 4, 4)].reshape(RANK, 128) for h in range(2)]
        parts = jnp.concatenate(split3(jnp.concatenate(tiles, axis=1)), axis=0)
        parts_buf[:, cols(at)] = parts
        return parts

    turned = (((1,), (1,)), ((), ()))
    acc = jnp.zeros((3 * RANK, COLS), F32)
    for i in range(STEPS // 2):
        part = slice(i * STEP, (i + 1) * STEP)
        parts = left_parts(core * (STEPS // 2) + i)
        acc = acc + lax.dot_general(parts, m_lo[:, part], turned, preferred_element_type=F32)
        acc = acc + lax.dot_general(parts, m_hi[:, part], turned, preferred_element_type=F32)
    acc = acc[2 * RANK :] + acc[RANK : 2 * RANK] + acc[0:RANK]
    q_part[:, :, 0:COLS] = acc.reshape(4, 8, COLS)
    q_part[:, :, COLS:] = jnp.zeros((4, 8, WIDE - COLS), F32)

    def owner(j, c):
        return j * 2 + c

    me = owner(member, core)
    partners = (
        (across, owner(1 - member, other)),
        (beside, owner(1 - member, core)),
        (sibling, owner(member, other)),
    )
    for n, (device, chunk) in enumerate(partners):
        pltpu.make_async_remote_copy(
            src_ref=q_part.at[chunk], dst_ref=d_rx.at[n],
            send_sem=d_send, recv_sem=d_recv, device_id=device, device_id_type=MESH,
        ).start()
    all_d = all_of(d_rx, d_send, d_recv)
    all_d.wait_recv()
    total = q_part[me] + d_rx[0] + d_rx[1] + d_rx[2]
    e_src[...] = total
    e_rx[group] = total
    for k in GROUPS:
        pltpu.make_async_remote_copy(
            src_ref=e_src, dst_ref=e_rx.at[group],
            send_sem=e_send, recv_sem=e_recv, device_id=group_peer(k), device_id_type=MESH,
        ).start()

    half_copy.wait_recv()
    for i in range(STEPS // 2):
        left_parts(other * (STEPS // 2) + i)
    gram = lax.dot_general(
        parts_buf[...], parts_buf[...], (((1,), (1,)), ((), ())), preferred_element_type=F32
    )
    gram = gram[2 * RANK :] + gram[RANK : 2 * RANK] + gram[0:RANK]
    gram = gram[:, 2 * RANK :] + gram[:, RANK : 2 * RANK] + gram[:, 0:RANK]

    row = lax.broadcasted_iota(jnp.int32, (RANK, 2 * RANK), 0)
    col = lax.broadcasted_iota(jnp.int32, (RANK, 2 * RANK), 1)
    unit = jnp.where(col == row + RANK, 1.0, 0.0).astype(F32)
    work = jnp.concatenate([gram, unit[:, RANK:]], axis=1)
    below = lax.broadcasted_iota(jnp.int32, (RANK, 1), 0)
    for k in range(RANK - 1):
        pivot = work[k : k + 1, :]
        factor = work[:, k : k + 1] / work[k : k + 1, k : k + 1]
        work = work - jnp.where(below > k, factor, 0.0) * pivot
    diagonal = jnp.sum(jnp.where(row == col, work, 0.0), axis=1, keepdims=True)
    inverse = work[:, RANK:] / jnp.sqrt(diagonal)

    for i in range(STEPS):
        tiles = [p_full[pl.ds(i * 8 + h * 4, 4)].reshape(RANK, 128) for h in range(2)]
        p_hat = jnp.dot(inverse, jnp.concatenate(tiles, axis=1), precision=HIGHEST, preferred_element_type=F32)
        p_out[:, cols(i)] = p_hat
        hi, mid, lo = split3(p_hat)
        p_split[:, cols(i)] = jnp.concatenate([hi, mid, hi, mid, lo, hi], axis=0)

    hi, mid, lo = split3(inverse)
    inverse_split = jnp.concatenate([hi, hi, mid, mid, hi, lo], axis=1)

    all_e = all_of(e_rx.at[pl.ds(0, 7)], e_send, e_recv)
    all_e.wait_recv()
    total = e_rx[0]
    for k in range(1, 8):
        total = total + e_rx[k]
    q_full[me] = total
    for n, (device, _) in enumerate(partners):
        pltpu.make_async_remote_copy(
            src_ref=q_full.at[me], dst_ref=q_full.at[me],
            send_sem=g_send, recv_sem=g_recv, device_id=device, device_id_type=MESH,
        ).start()
    all_g = all_of(q_full.at[pl.ds(0, 3)], g_send, g_recv)
    all_g.wait_recv()
    q_sum = q_full[...].reshape(RANK, WIDE)
    hi, mid, lo = split3(q_sum)
    q_stack = jnp.concatenate([hi, mid, hi, mid, lo, hi], axis=0)
    q_new = jnp.dot(inverse_split, q_stack, preferred_element_type=F32) * (1.0 / 32.0)
    q_out[...] = q_new[:, 0:COLS]
    core_copy.wait_send()
    all_a.wait_send()
    all_b.wait_send()
    all_c.wait_send()
    half_copy.wait_send()
    for i in range(STEPS // 2):
        swap(i).wait_send()
    all_d.wait_send()
    all_e.wait_send()
    all_g.wait_send()


def update_kernel(merged, p_split, p_hat, q_new, new_errors, p_out, q_out, stage, out_sem, side_sem):
    p_copy = pltpu.make_async_copy(p_hat, p_out, side_sem.at[0])
    q_copy = pltpu.make_async_copy(q_new, q_out, side_sem.at[1])
    p_copy.start()
    q_copy.start()
    hi, mid, lo = split3(q_new[...].T)
    q_split = jnp.concatenate([hi, hi, mid, mid, hi, lo], axis=1)

    def store(i):
        at = pl.ds(i * STEP, STEP)
        return pltpu.make_async_copy(stage.at[:, at], new_errors.at[:, at], out_sem.at[i])

    for i in range(STEPS):
        at = pl.ds(i * STEP, STEP)
        delta = jnp.dot(q_split, p_split[:, at], preferred_element_type=F32)
        stage[:, at] = (merged[:, at].astype(F32) - delta).astype(BF16)
        store(i).start()
    p_copy.wait()
    q_copy.wait()
    for i in range(STEPS):
        store(i).wait()


def body(grads, errors, q_start):
    hbm_spec = pl.BlockSpec(memory_space=pltpu.HBM)
    vmem_spec = pl.BlockSpec(memory_space=pltpu.VMEM)
    dma = pltpu.SemaphoreType.DMA
    tile = (8, 128)
    strip = (8, WIDE)
    merged, p_split, p_hat, q_new = pl.pallas_call(
        kernel,
        name="factors",
        out_shape=(
            jax.ShapeDtypeStruct((COLS, ROWS), BF16),
            jax.ShapeDtypeStruct((6 * RANK, ROWS), BF16),
            jax.ShapeDtypeStruct((RANK, ROWS), F32),
            jax.ShapeDtypeStruct((RANK, COLS), F32),
        ),
        in_specs=[hbm_spec, hbm_spec, hbm_spec],
        out_specs=(vmem_spec,) * 4,
        scratch_shapes=[
            pltpu.VMEM((RANK, COLS), F32),
            pltpu.VMEM((COLS, ROWS), BF16),
            pltpu.VMEM((COLS, ROWS), BF16),
            pltpu.VMEM((3 * RANK, ROWS), BF16),
            pltpu.VMEM((64,) + tile, F32),
            pltpu.VMEM((32,) + tile, F32),
            pltpu.VMEM((32,) + tile, F32),
            pltpu.VMEM((31,) + tile, F32),
            pltpu.VMEM(tile, F32),
            pltpu.VMEM((8,) + tile, F32),
            pltpu.VMEM((64,) + tile, F32),
            pltpu.VMEM((4,) + strip, F32),
            pltpu.VMEM((3,) + strip, F32),
            pltpu.VMEM(strip, F32),
            pltpu.VMEM((8,) + strip, F32),
            pltpu.VMEM((4,) + strip, F32),
            pltpu.VMEM((COLS, ROWS // 2), F32),
            pltpu.VMEM((COLS, ROWS // 2), F32),
            pltpu.VMEM((COLS, ROWS // 2), BF16),
            pltpu.VMEM((COLS, ROWS // 2), BF16),
            pltpu.SemaphoreType.REGULAR,
            dma((STEPS // 2,)),
            dma((STEPS // 2,)),
            dma,
            dma((2, STEPS)),
        ]
        + [dma] * 16,
        compiler_params=pltpu.CompilerParams(
            collective_id=0, has_side_effects=True, vmem_limit_bytes=32 * 1024 * 1024
        ),
    )(*(pltpu.with_memory_space_constraint(a, pltpu.HBM) for a in (grads[0].T, errors[0].T, q_start.T)))
    new_errors, p_hat, q_new = pl.pallas_call(
        update_kernel,
        name="update",
        out_shape=(
            jax.ShapeDtypeStruct((COLS, ROWS), BF16),
            jax.ShapeDtypeStruct((RANK, ROWS), F32),
            jax.ShapeDtypeStruct((RANK, COLS), F32),
        ),
        in_specs=[vmem_spec] * 4,
        out_specs=(hbm_spec,) * 3,
        scratch_shapes=[pltpu.VMEM((COLS, ROWS), BF16), dma((STEPS,)), dma((2,))],
        compiler_params=pltpu.CompilerParams(vmem_limit_bytes=16 * 1024 * 1024),
    )(merged, p_split, p_hat, q_new)
    return new_errors.T[None], p_hat.T, q_new.T


def solution(mesh):
    placed = (P("dp", None, "tensor"), P("dp", None, "tensor"), P("tensor", None))
    return jax.shard_map(
        body,
        mesh=mesh,
        in_specs=placed,
        out_specs=(P("dp", None, "tensor"), P(), P("tensor", None)),
        check_vma=False,
    )
```

```python
import functools

import jax
import jax.numpy as jnp
from jax import lax
from jax.experimental import pallas as pl
from jax.experimental.pallas import tpu as pltpu
from jax.sharding import PartitionSpec as P

MESH = pl.DeviceIdType.MESH
HIGHEST = lax.Precision.HIGHEST
F32, BF16 = jnp.float32, jnp.bfloat16

RANK = 32
ROWS = 2048
COLS = 352
WIDE = 384
STEP = 256
STEPS = ROWS // STEP

FAR = {0: 0, 1: 1, 2: 2, 3: 1}
OFFSETS = sorted(
    ((j, y, x) for j in range(2) for y in range(4) for x in range(4) if (j, y, x) != (0, 0, 0)),
    key=lambda o: -(o[0] + FAR[o[1]] + FAR[o[2]]),
)
GROUPS = [4, 3, 5, 2, 6, 1, 7]


def split3(value):
    hi = value.astype(BF16)
    rest = value - hi.astype(F32)
    mid = rest.astype(BF16)
    lo = (rest - mid.astype(F32)).astype(BF16)
    return hi, mid, lo


def kernel(
    grads, errors, q_start, merged_out, p_split, p_out, q_out,
    q_in, gbuf, ebuf, parts_buf, pt, core_rx, a_src, a_rx, b_src, b_rx, p_full,
    q_part, d_rx, e_src, e_rx, q_full, m_src, m_rx, m_hi, m_lo,
    ready, m_send, m_recv, q_sem, load_sem, core_send, core_recv, a_send, a_recv, b_send, b_recv, c_send, c_recv,
    f_send, f_recv, d_send, d_recv, e_send, e_recv, g_send, g_recv,
):
    dp, tensor = lax.axis_index("dp"), lax.axis_index("tensor")
    z, core = lax.div(dp, 2), lax.rem(dp, 2)
    group, bit = lax.div(z, 2), lax.rem(z, 2)
    member = lax.rem(bit + lax.div(group, 4), 2)
    y, x = lax.div(tensor, 4), lax.rem(tensor, 4)
    columns_of = [lax.rem(x + k, 4) for k in range(4)]
    rows_of = [lax.rem(y + k, 4) * 4 for k in range(4)]
    members = [member, 1 - member]
    in_pair = [dp, 4 * group + 2 * (1 - bit) + core]

    def plane_peer(o):
        t = rows_of[o[1]] + columns_of[o[2]]
        return (in_pair[o[0]], t), members[o[0]] * 16 + t

    def group_at(a):
        return (4 * a + 2 * (member if a < 4 else 1 - member) + core, tensor)

    def group_peer(k):
        a = lax.rem(group + k, 8)
        return (4 * a + 2 * lax.rem(member + lax.div(a, 4), 2) + core, tensor)

    other = 1 - core
    sibling = (dp + other - core, tensor)
    beside = (in_pair[1], tensor)
    across = (in_pair[1] + other - core, tensor)
    mine = member * 16 + tensor

    def cols(i):
        return pl.ds(pl.multiple_of(i * STEP, STEP), STEP)

    def half_at(i):
        return (other if i < STEPS // 2 else core) * (STEPS // 2) + i % (STEPS // 2)

    def load(i):
        at = half_at(i)
        return (
            pltpu.make_async_copy(grads.at[:, cols(at)], gbuf.at[:, cols(at)], load_sem.at[0, i]),
            pltpu.make_async_copy(errors.at[:, cols(at)], ebuf.at[:, cols(at)], load_sem.at[1, i]),
        )

    q_copy = pltpu.make_async_copy(q_start, q_in, q_sem)
    q_copy.start()
    for i in range(2):
        for copy in load(i):
            copy.start()

    barrier = pltpu.get_barrier_semaphore()
    for a in range(8):

        @pl.when(group < a)
        def _():
            pl.semaphore_signal(barrier, inc=1, device_id=group_at(a), device_id_type=MESH)

    for o in OFFSETS:
        pl.semaphore_signal(barrier, inc=1, device_id=plane_peer(o)[0], device_id_type=MESH)
    pl.semaphore_signal(barrier, inc=1, device_id=across, device_id_type=MESH)
    pl.semaphore_signal(barrier, inc=1, device_id=sibling, device_id_type=MESH)

    for i in range(2, STEPS):
        for copy in load(i):
            copy.start()
    q_copy.wait()
    q_narrow = q_in[...].astype(BF16)

    def left(i):
        for copy in load(i):
            copy.wait()
        at = half_at(i)
        merged = (gbuf[:, cols(at)].astype(F32) + ebuf[:, cols(at)].astype(F32)).astype(BF16)
        merged_out[:, cols(at)] = merged
        part = jnp.dot(q_narrow, merged, preferred_element_type=F32)
        for h in range(2):
            pt[pl.ds(at * 8 + h * 4, 4)] = part[:, h * 128 : (h + 1) * 128].reshape(4, 8, 128)

    for i in range(STEPS // 2):
        left(i)
    pl.semaphore_wait(barrier, len(OFFSETS) + 2 + group)
    for a in range(8):

        @pl.when(group > a)
        def _():
            pl.semaphore_signal(ready, inc=1, device_id=group_at(a), device_id_type=MESH)

    core_copy = pltpu.make_async_remote_copy(
        src_ref=pt.at[pl.ds(other * 32, 32)], dst_ref=core_rx,
        send_sem=core_send, recv_sem=core_recv, device_id=sibling, device_id_type=MESH,
    )
    core_copy.start()
    for i in range(STEPS // 2, STEPS):
        left(i)
    core_copy.wait_recv()
    a_src[...] = pt[pl.ds(core * 32, 32)] + core_rx[...]

    for n, o in enumerate(OFFSETS):
        device, chunk = plane_peer(o)
        pltpu.make_async_remote_copy(
            src_ref=a_src.at[chunk], dst_ref=a_rx.at[n],
            send_sem=a_send, recv_sem=a_recv, device_id=device, device_id_type=MESH,
        ).start()

    def swap(i):
        part = pl.ds(i * STEP, STEP)
        return pltpu.make_async_remote_copy(
            src_ref=m_src.at[:, part], dst_ref=m_rx.at[:, part],
            send_sem=m_send.at[i], recv_sem=m_recv.at[i], device_id=sibling, device_id_type=MESH,
        )

    for i in range(STEPS // 2):
        m_src[:, i * STEP : (i + 1) * STEP] = merged_out[:, cols(half_at(i))].astype(F32)
        swap(i).start()

    def all_of(ref, send, recv):
        return pltpu.make_async_remote_copy(
            src_ref=ref, dst_ref=ref, send_sem=send, recv_sem=recv, device_id=sibling, device_id_type=MESH
        )

    all_a = all_of(a_rx, a_send, a_recv)
    all_a.wait_recv()
    total = a_src[mine]
    for n in range(len(OFFSETS)):
        total = total + a_rx[n]
    b_src[...] = total
    b_rx[group] = total

    def spread(a):
        pltpu.make_async_remote_copy(
            src_ref=b_src, dst_ref=b_rx.at[group],
            send_sem=b_send, recv_sem=b_recv, device_id=group_at(a), device_id_type=MESH,
        ).start()

    for a in range(7):

        @pl.when(group > a)
        def _():
            spread(a)

    @pl.when(group < 7)
    def _():
        pl.semaphore_wait(ready, 7 - group)

    for a in range(7, 0, -1):

        @pl.when(group < a)
        def _():
            spread(a)

    for i in range(STEPS // 2):
        part = slice(i * STEP, (i + 1) * STEP)
        swap(i).wait_recv()
        both = merged_out[:, cols(core * (STEPS // 2) + i)].astype(F32) + m_rx[:, part]
        hi = both.astype(BF16)
        m_hi[:, part] = hi
        m_lo[:, part] = (both - hi.astype(F32)).astype(BF16)

    all_b = all_of(b_rx.at[pl.ds(0, 7)], b_send, b_recv)
    all_b.wait_recv()
    total = b_rx[0]
    for k in range(1, 8):
        total = total + b_rx[k]
    p_full[core * 32 + mine] = total
    batch = lax.div(mine, 8)

    for n, o in enumerate(OFFSETS):
        pltpu.make_async_remote_copy(
            src_ref=p_full.at[core * 32 + mine], dst_ref=p_full.at[core * 32 + mine],
            send_sem=c_send, recv_sem=c_recv.at[batch], device_id=plane_peer(o)[0], device_id_type=MESH,
        ).start()
    def left_parts(at):
        tiles = [p_full[pl.ds(at * 8 + h * 4, 4)].reshape(RANK, 128) for h in range(2)]
        parts = jnp.concatenate(split3(jnp.concatenate(tiles, axis=1)), axis=0)
        parts_buf[:, cols(at)] = parts
        return parts

    turned = (((1,), (1,)), ((), ()))
    acc = jnp.zeros((3 * RANK, COLS), F32)
    for i in range(STEPS // 2):
        this = lax.rem(member * 2 + i, 4)

        @pl.when(batch == this)
        def _():
            all_of(p_full.at[pl.ds(0, 7)], c_send, c_recv.at[this]).wait_recv()

        @pl.when(batch != this)
        def _():
            all_of(p_full.at[pl.ds(0, 8)], c_send, c_recv.at[this]).wait_recv()

        parts = left_parts(core * (STEPS // 2) + this)
        acc = acc + lax.dot_general(parts, m_lo[:, cols(this)], turned, preferred_element_type=F32)
        acc = acc + lax.dot_general(parts, m_hi[:, cols(this)], turned, preferred_element_type=F32)
    half = pl.ds(core * 32, 32)
    half_copy = pltpu.make_async_remote_copy(
        src_ref=p_full.at[half], dst_ref=p_full.at[half],
        send_sem=f_send, recv_sem=f_recv, device_id=sibling, device_id_type=MESH,
    )
    half_copy.start()
    acc = acc[2 * RANK :] + acc[RANK : 2 * RANK] + acc[0:RANK]
    q_part[:, :, 0:COLS] = acc.reshape(4, 8, COLS)
    q_part[:, :, COLS:] = jnp.zeros((4, 8, WIDE - COLS), F32)

    def owner(j, c):
        return j * 2 + c

    me = owner(member, core)
    partners = (
        (across, owner(1 - member, other)),
        (beside, owner(1 - member, core)),
        (sibling, owner(member, other)),
    )
    for n, (device, chunk) in enumerate(partners):
        pltpu.make_async_remote_copy(
            src_ref=q_part.at[chunk], dst_ref=d_rx.at[n],
            send_sem=d_send, recv_sem=d_recv, device_id=device, device_id_type=MESH,
        ).start()
    all_d = all_of(d_rx, d_send, d_recv)
    all_d.wait_recv()
    total = q_part[me] + d_rx[0] + d_rx[1] + d_rx[2]
    e_src[...] = total
    e_rx[group] = total
    for k in GROUPS:
        pltpu.make_async_remote_copy(
            src_ref=e_src, dst_ref=e_rx.at[group],
            send_sem=e_send, recv_sem=e_recv, device_id=group_peer(k), device_id_type=MESH,
        ).start()

    half_copy.wait_recv()
    for i in range(STEPS // 2):
        left_parts(other * (STEPS // 2) + i)
    gram = lax.dot_general(
        parts_buf[...], parts_buf[...], (((1,), (1,)), ((), ())), preferred_element_type=F32
    )
    gram = gram[2 * RANK :] + gram[RANK : 2 * RANK] + gram[0:RANK]
    gram = gram[:, 2 * RANK :] + gram[:, RANK : 2 * RANK] + gram[:, 0:RANK]

    row = lax.broadcasted_iota(jnp.int32, (RANK, 2 * RANK), 0)
    col = lax.broadcasted_iota(jnp.int32, (RANK, 2 * RANK), 1)
    unit = jnp.where(col == row + RANK, 1.0, 0.0).astype(F32)
    work = jnp.concatenate([gram, unit[:, RANK:]], axis=1)
    below = lax.broadcasted_iota(jnp.int32, (RANK, 1), 0)
    for k in range(RANK - 1):
        pivot = work[k : k + 1, :]
        factor = work[:, k : k + 1] / work[k : k + 1, k : k + 1]
        work = work - jnp.where(below > k, factor, 0.0) * pivot
    diagonal = jnp.sum(jnp.where(row == col, work, 0.0), axis=1, keepdims=True)
    inverse = work[:, RANK:] / jnp.sqrt(diagonal)

    for i in range(STEPS):
        tiles = [p_full[pl.ds(i * 8 + h * 4, 4)].reshape(RANK, 128) for h in range(2)]
        p_hat = jnp.dot(inverse, jnp.concatenate(tiles, axis=1), precision=HIGHEST, preferred_element_type=F32)
        p_out[:, cols(i)] = p_hat
        hi, mid, _ = split3(p_hat)
        p_split[:, cols(i)] = jnp.concatenate([hi, hi, mid], axis=0)

    hi, mid, lo = split3(inverse)
    inverse_split = jnp.concatenate([hi, hi, mid, mid, hi, lo], axis=1)

    all_e = all_of(e_rx.at[pl.ds(0, 7)], e_send, e_recv)
    all_e.wait_recv()
    total = e_rx[0]
    for k in range(1, 8):
        total = total + e_rx[k]
    q_full[me] = total
    for n, (device, _) in enumerate(partners):
        pltpu.make_async_remote_copy(
            src_ref=q_full.at[me], dst_ref=q_full.at[me],
            send_sem=g_send, recv_sem=g_recv, device_id=device, device_id_type=MESH,
        ).start()
    all_g = all_of(q_full.at[pl.ds(0, 3)], g_send, g_recv)
    all_g.wait_recv()
    q_sum = q_full[...].reshape(RANK, WIDE)
    hi, mid, lo = split3(q_sum)
    q_stack = jnp.concatenate([hi, mid, hi, mid, lo, hi], axis=0)
    q_new = jnp.dot(inverse_split, q_stack, preferred_element_type=F32) * (1.0 / 32.0)
    q_out[...] = q_new[:, 0:COLS]
    core_copy.wait_send()
    all_a.wait_send()
    all_b.wait_send()
    all_of(p_full.at[pl.ds(0, 31)], c_send, c_recv.at[0]).wait_send()
    half_copy.wait_send()
    for i in range(STEPS // 2):
        swap(i).wait_send()
    all_d.wait_send()
    all_e.wait_send()
    all_g.wait_send()


def update_kernel(merged, p_split, p_hat, q_new, new_errors, p_out, q_out, stage, out_sem, side_sem):
    p_copy = pltpu.make_async_copy(p_hat, p_out, side_sem.at[0])
    q_copy = pltpu.make_async_copy(q_new, q_out, side_sem.at[1])
    p_copy.start()
    q_copy.start()
    hi, mid, _ = split3(q_new[...].T)
    q_split = jnp.concatenate([hi, mid, hi], axis=1)

    def store(i):
        at = pl.ds(i * STEP, STEP)
        return pltpu.make_async_copy(stage.at[:, at], new_errors.at[:, at], out_sem.at[i])

    for i in range(STEPS):
        at = pl.ds(i * STEP, STEP)
        delta = jnp.dot(q_split, p_split[:, at], preferred_element_type=F32)
        stage[:, at] = (merged[:, at].astype(F32) - delta).astype(BF16)
        store(i).start()
    p_copy.wait()
    q_copy.wait()
    for i in range(STEPS):
        store(i).wait()


def body(grads, errors, q_start):
    hbm_spec = pl.BlockSpec(memory_space=pltpu.HBM)
    vmem_spec = pl.BlockSpec(memory_space=pltpu.VMEM)
    dma = pltpu.SemaphoreType.DMA
    tile = (8, 128)
    strip = (8, WIDE)
    merged, p_split, p_hat, q_new = pl.pallas_call(
        kernel,
        name="factors",
        out_shape=(
            jax.ShapeDtypeStruct((COLS, ROWS), BF16),
            jax.ShapeDtypeStruct((3 * RANK, ROWS), BF16),
            jax.ShapeDtypeStruct((RANK, ROWS), F32),
            jax.ShapeDtypeStruct((RANK, COLS), F32),
        ),
        in_specs=[hbm_spec, hbm_spec, hbm_spec],
        out_specs=(vmem_spec,) * 4,
        scratch_shapes=[
            pltpu.VMEM((RANK, COLS), F32),
            pltpu.VMEM((COLS, ROWS), BF16),
            pltpu.VMEM((COLS, ROWS), BF16),
            pltpu.VMEM((3 * RANK, ROWS), BF16),
            pltpu.VMEM((64,) + tile, F32),
            pltpu.VMEM((32,) + tile, F32),
            pltpu.VMEM((32,) + tile, F32),
            pltpu.VMEM((31,) + tile, F32),
            pltpu.VMEM(tile, F32),
            pltpu.VMEM((8,) + tile, F32),
            pltpu.VMEM((64,) + tile, F32),
            pltpu.VMEM((4,) + strip, F32),
            pltpu.VMEM((3,) + strip, F32),
            pltpu.VMEM(strip, F32),
            pltpu.VMEM((8,) + strip, F32),
            pltpu.VMEM((4,) + strip, F32),
            pltpu.VMEM((COLS, ROWS // 2), F32),
            pltpu.VMEM((COLS, ROWS // 2), F32),
            pltpu.VMEM((COLS, ROWS // 2), BF16),
            pltpu.VMEM((COLS, ROWS // 2), BF16),
            pltpu.SemaphoreType.REGULAR,
            dma((STEPS // 2,)),
            dma((STEPS // 2,)),
            dma,
            dma((2, STEPS)),
        ]
        + [dma] * 7
        + [dma((4,))]
        + [dma] * 8,
        compiler_params=pltpu.CompilerParams(
            collective_id=0, has_side_effects=True, vmem_limit_bytes=32 * 1024 * 1024
        ),
    )(*(pltpu.with_memory_space_constraint(a, pltpu.HBM) for a in (grads[0].T, errors[0].T, q_start.T)))
    new_errors, p_hat, q_new = pl.pallas_call(
        update_kernel,
        name="update",
        out_shape=(
            jax.ShapeDtypeStruct((COLS, ROWS), BF16),
            jax.ShapeDtypeStruct((RANK, ROWS), F32),
            jax.ShapeDtypeStruct((RANK, COLS), F32),
        ),
        in_specs=[vmem_spec] * 4,
        out_specs=(hbm_spec,) * 3,
        scratch_shapes=[pltpu.VMEM((COLS, ROWS), BF16), dma((STEPS,)), dma((2,))],
        compiler_params=pltpu.CompilerParams(vmem_limit_bytes=16 * 1024 * 1024),
    )(merged, p_split, p_hat, q_new)
    return new_errors.T[None], p_hat.T, q_new.T


def solution(mesh):
    placed = (P("dp", None, "tensor"), P("dp", None, "tensor"), P("tensor", None))
    return jax.shard_map(
        body,
        mesh=mesh,
        in_specs=placed,
        out_specs=(P("dp", None, "tensor"), P(), P("tensor", None)),
        check_vma=False,
    )
```

```python
import functools

import jax
import jax.numpy as jnp
from jax import lax
from jax.experimental import pallas as pl
from jax.experimental.pallas import tpu as pltpu
from jax.sharding import PartitionSpec as P

MESH = pl.DeviceIdType.MESH
HIGHEST = lax.Precision.HIGHEST
F32, BF16 = jnp.float32, jnp.bfloat16

RANK = 32
ROWS = 2048
COLS = 352
WIDE = 384
STEP = 256
STEPS = ROWS // STEP
STRIDE = 512

FAR = {0: 0, 1: 1, 2: 2, 3: 1}
OFFSETS = sorted(
    ((j, y, x) for j in range(2) for y in range(4) for x in range(4) if (j, y, x) != (0, 0, 0)),
    key=lambda o: -(o[0] + FAR[o[1]] + FAR[o[2]]),
)
GROUPS = [4, 3, 5, 2, 6, 1, 7]


def split3(value):
    hi = value.astype(BF16)
    rest = value - hi.astype(F32)
    mid = rest.astype(BF16)
    lo = (rest - mid.astype(F32)).astype(BF16)
    return hi, mid, lo


def kernel(
    grads, errors, q_start, merged_out, p_split, p_out, q_out,
    q_in, gbuf, ebuf, parts_buf, pt, core_rx, a_src, a_rx, b_src, b_rx, p_full,
    q_part, d_rx, e_src, e_rx, q_full, m_src, m_rx, m_hi, m_lo,
    ready, m_send, m_recv, q_sem, load_sem, core_send, core_recv, a_send, a_recv, b_send, b_recv, c_send, c_recv,
    f_send, f_recv, d_send, d_recv, e_send, e_recv, g_send, g_recv,
):
    dp, tensor = lax.axis_index("dp"), lax.axis_index("tensor")
    z, core = lax.div(dp, 2), lax.rem(dp, 2)
    group, bit = lax.div(z, 2), lax.rem(z, 2)
    member = lax.rem(bit + lax.div(group, 4), 2)
    y, x = lax.div(tensor, 4), lax.rem(tensor, 4)
    columns_of = [lax.rem(x + k, 4) for k in range(4)]
    rows_of = [lax.rem(y + k, 4) * 4 for k in range(4)]
    members = [member, 1 - member]
    in_pair = [dp, 4 * group + 2 * (1 - bit) + core]

    def plane_peer(o):
        t = rows_of[o[1]] + columns_of[o[2]]
        return (in_pair[o[0]], t), members[o[0]] * 16 + t

    def group_at(a):
        return (4 * a + 2 * (member if a < 4 else 1 - member) + core, tensor)

    def group_peer(k):
        a = lax.rem(group + k, 8)
        return (4 * a + 2 * lax.rem(member + lax.div(a, 4), 2) + core, tensor)

    other = 1 - core
    sibling = (dp + other - core, tensor)
    beside = (in_pair[1], tensor)
    across = (in_pair[1] + other - core, tensor)
    mine = member * 16 + tensor

    def cols(i):
        return pl.ds(pl.multiple_of(i * STEP, STEP), STEP)

    def half_at(i):
        return (other if i < STEPS // 2 else core) * (STEPS // 2) + i % (STEPS // 2)

    def load(i):
        at = half_at(i)
        return (
            pltpu.make_async_copy(grads.at[:, cols(at)], gbuf.at[:, cols(at)], load_sem.at[0, i]),
            pltpu.make_async_copy(errors.at[:, cols(at)], ebuf.at[:, cols(at)], load_sem.at[1, i]),
        )

    q_copy = pltpu.make_async_copy(q_start, q_in, q_sem)
    q_copy.start()
    for i in range(2):
        for copy in load(i):
            copy.start()

    barrier = pltpu.get_barrier_semaphore()
    for a in range(8):

        @pl.when(group < a)
        def _():
            pl.semaphore_signal(barrier, inc=1, device_id=group_at(a), device_id_type=MESH)

    for o in OFFSETS:
        pl.semaphore_signal(barrier, inc=1, device_id=plane_peer(o)[0], device_id_type=MESH)
    pl.semaphore_signal(barrier, inc=1, device_id=across, device_id_type=MESH)
    pl.semaphore_signal(barrier, inc=1, device_id=sibling, device_id_type=MESH)

    for i in range(2, STEPS):
        for copy in load(i):
            copy.start()
    q_copy.wait()
    q_narrow = q_in[...].astype(BF16)

    def left(i):
        for copy in load(i):
            copy.wait()
        at = half_at(i)
        merged = (gbuf[:, cols(at)].astype(F32) + ebuf[:, cols(at)].astype(F32)).astype(BF16)
        merged_out[:, cols(at)] = merged
        part = jnp.dot(q_narrow, merged, preferred_element_type=F32)
        for h in range(2):
            pt[pl.ds(at * 8 + h * 4, 4)] = part[:, h * 128 : (h + 1) * 128].reshape(4, 8, 128)

    for i in range(STEPS):
        left(i)
    pl.semaphore_wait(barrier, len(OFFSETS) + 2 + group)
    for a in range(8):

        @pl.when(group > a)
        def _():
            pl.semaphore_signal(ready, inc=1, device_id=group_at(a), device_id_type=MESH)

    core_copy = pltpu.make_async_remote_copy(
        src_ref=pt.at[pl.ds(other * 32, 32)], dst_ref=core_rx,
        send_sem=core_send, recv_sem=core_recv, device_id=sibling, device_id_type=MESH,
    )
    core_copy.start()
    for i in range(STEPS // 2):
        m_src[:, i * STEP : (i + 1) * STEP] = merged_out[:, cols(half_at(i))].astype(F32)
    core_copy.wait_recv()
    a_src[...] = pt[pl.ds(core * 32, 32)] + core_rx[...]

    for n, o in enumerate(OFFSETS):
        device, chunk = plane_peer(o)
        pltpu.make_async_remote_copy(
            src_ref=a_src.at[chunk], dst_ref=a_rx.at[n],
            send_sem=a_send, recv_sem=a_recv, device_id=device, device_id_type=MESH,
        ).start()

    def swap(i):
        part = pl.ds(i * STEP, STEP)
        return pltpu.make_async_remote_copy(
            src_ref=m_src.at[:, part], dst_ref=m_rx.at[:, part],
            send_sem=m_send.at[i], recv_sem=m_recv.at[i], device_id=sibling, device_id_type=MESH,
        )

    for i in range(STEPS // 2):
        swap(i).start()

    def all_of(ref, send, recv):
        return pltpu.make_async_remote_copy(
            src_ref=ref, dst_ref=ref, send_sem=send, recv_sem=recv, device_id=sibling, device_id_type=MESH
        )

    all_a = all_of(a_rx, a_send, a_recv)
    all_a.wait_recv()
    total = a_src[mine]
    for n in range(len(OFFSETS)):
        total = total + a_rx[n]
    b_src[...] = total
    b_rx[group] = total

    def spread(a):
        pltpu.make_async_remote_copy(
            src_ref=b_src, dst_ref=b_rx.at[group],
            send_sem=b_send, recv_sem=b_recv, device_id=group_at(a), device_id_type=MESH,
        ).start()

    for a in range(7):

        @pl.when(group > a)
        def _():
            spread(a)

    @pl.when(group < 7)
    def _():
        pl.semaphore_wait(ready, 7 - group)

    for a in range(7, 0, -1):

        @pl.when(group < a)
        def _():
            spread(a)

    for i in range(STEPS // 2):
        part = slice(i * STEP, (i + 1) * STEP)
        swap(i).wait_recv()
        both = merged_out[:, cols(core * (STEPS // 2) + i)].astype(F32) + m_rx[:, part]
        hi = both.astype(BF16)
        m_hi[:, part] = hi
        m_lo[:, part] = (both - hi.astype(F32)).astype(BF16)

    all_b = all_of(b_rx.at[pl.ds(0, 7)], b_send, b_recv)
    all_b.wait_recv()
    total = b_rx[0]
    for k in range(1, 8):
        total = total + b_rx[k]
    p_full[core * 32 + mine] = total
    batch = lax.div(mine, 8)

    for n, o in enumerate(OFFSETS):
        pltpu.make_async_remote_copy(
            src_ref=p_full.at[core * 32 + mine], dst_ref=p_full.at[core * 32 + mine],
            send_sem=c_send, recv_sem=c_recv.at[batch], device_id=plane_peer(o)[0], device_id_type=MESH,
        ).start()
    def left_parts(at):
        tiles = [p_full[pl.ds(at * 8 + h * 4, 4)].reshape(RANK, 128) for h in range(2)]
        parts = jnp.concatenate(split3(jnp.concatenate(tiles, axis=1)), axis=0)
        parts_buf[:, cols(at)] = parts
        return parts

    turned = (((1,), (1,)), ((), ()))
    acc = jnp.zeros((3 * RANK, COLS), F32)
    for i in range(STEPS // 2):
        this = lax.rem(member * 2 + i, 4)

        @pl.when(batch == this)
        def _():
            all_of(p_full.at[pl.ds(0, 7)], c_send, c_recv.at[this]).wait_recv()

        @pl.when(batch != this)
        def _():
            all_of(p_full.at[pl.ds(0, 8)], c_send, c_recv.at[this]).wait_recv()

        parts = left_parts(core * (STEPS // 2) + this)
        acc = acc + lax.dot_general(parts, m_lo[:, cols(this)], turned, preferred_element_type=F32)
        acc = acc + lax.dot_general(parts, m_hi[:, cols(this)], turned, preferred_element_type=F32)
    half = pl.ds(core * 32, 32)
    half_copy = pltpu.make_async_remote_copy(
        src_ref=p_full.at[half], dst_ref=p_full.at[half],
        send_sem=f_send, recv_sem=f_recv, device_id=sibling, device_id_type=MESH,
    )
    half_copy.start()
    acc = acc[2 * RANK :] + acc[RANK : 2 * RANK] + acc[0:RANK]
    q_part[:, :, 0:COLS] = acc.reshape(4, 8, COLS)
    q_part[:, :, COLS:] = jnp.zeros((4, 8, WIDE - COLS), F32)

    def owner(j, c):
        return j * 2 + c

    me = owner(member, core)
    partners = (
        (across, owner(1 - member, other)),
        (beside, owner(1 - member, core)),
        (sibling, owner(member, other)),
    )
    for n, (device, chunk) in enumerate(partners):
        pltpu.make_async_remote_copy(
            src_ref=q_part.at[chunk], dst_ref=d_rx.at[n],
            send_sem=d_send, recv_sem=d_recv, device_id=device, device_id_type=MESH,
        ).start()
    all_d = all_of(d_rx, d_send, d_recv)
    all_d.wait_recv()
    total = q_part[me] + d_rx[0] + d_rx[1] + d_rx[2]
    e_src[...] = total
    e_rx[group] = total
    for k in GROUPS:
        pltpu.make_async_remote_copy(
            src_ref=e_src, dst_ref=e_rx.at[group],
            send_sem=e_send, recv_sem=e_recv, device_id=group_peer(k), device_id_type=MESH,
        ).start()

    half_copy.wait_recv()
    for i in range(STEPS // 2):
        left_parts(other * (STEPS // 2) + i)
    gram = lax.dot_general(
        parts_buf[...], parts_buf[...], (((1,), (1,)), ((), ())), preferred_element_type=F32
    )
    gram = gram[2 * RANK :] + gram[RANK : 2 * RANK] + gram[0:RANK]
    gram = gram[:, 2 * RANK :] + gram[:, RANK : 2 * RANK] + gram[:, 0:RANK]

    row = lax.broadcasted_iota(jnp.int32, (RANK, 2 * RANK), 0)
    col = lax.broadcasted_iota(jnp.int32, (RANK, 2 * RANK), 1)
    unit = jnp.where(col == row + RANK, 1.0, 0.0).astype(F32)
    work = jnp.concatenate([gram, unit[:, RANK:]], axis=1)
    below = lax.broadcasted_iota(jnp.int32, (RANK, 1), 0)
    for k in range(RANK - 1):
        pivot = work[k : k + 1, :]
        factor = work[:, k : k + 1] / work[k : k + 1, k : k + 1]
        work = work - jnp.where(below > k, factor, 0.0) * pivot
    diagonal = jnp.sum(jnp.where(row == col, work, 0.0), axis=1, keepdims=True)
    inverse = work[:, RANK:] / jnp.sqrt(diagonal)

    for i in range(STEPS):
        tiles = [p_full[pl.ds(i * 8 + h * 4, 4)].reshape(RANK, 128) for h in range(2)]
        p_hat = jnp.dot(inverse, jnp.concatenate(tiles, axis=1), precision=HIGHEST, preferred_element_type=F32)
        p_out[:, cols(i)] = p_hat
        hi, mid, _ = split3(p_hat)
        p_split[:, cols(i)] = jnp.concatenate([hi, hi, mid], axis=0)

    hi, mid, lo = split3(inverse)
    inverse_split = jnp.concatenate([hi, hi, mid, mid, hi, lo], axis=1)

    all_e = all_of(e_rx.at[pl.ds(0, 7)], e_send, e_recv)
    all_e.wait_recv()
    total = e_rx[0]
    for k in range(1, 8):
        total = total + e_rx[k]
    q_full[me] = total
    for n, (device, _) in enumerate(partners):
        pltpu.make_async_remote_copy(
            src_ref=q_full.at[me], dst_ref=q_full.at[me],
            send_sem=g_send, recv_sem=g_recv, device_id=device, device_id_type=MESH,
        ).start()
    all_g = all_of(q_full.at[pl.ds(0, 3)], g_send, g_recv)
    all_g.wait_recv()
    q_sum = q_full[...].reshape(RANK, WIDE)
    hi, mid, lo = split3(q_sum)
    q_stack = jnp.concatenate([hi, mid, hi, mid, lo, hi], axis=0)
    q_new = jnp.dot(inverse_split, q_stack, preferred_element_type=F32) * (1.0 / 32.0)
    q_out[...] = q_new[:, 0:COLS]
    core_copy.wait_send()
    all_a.wait_send()
    all_b.wait_send()
    all_of(p_full.at[pl.ds(0, 31)], c_send, c_recv.at[0]).wait_send()
    half_copy.wait_send()
    for i in range(STEPS // 2):
        swap(i).wait_send()
    all_d.wait_send()
    all_e.wait_send()
    all_g.wait_send()


def update_kernel(merged, p_split, p_hat, q_new, new_errors, p_out, q_out, stage, out_sem, side_sem):
    p_copy = pltpu.make_async_copy(p_hat, p_out, side_sem.at[0])
    q_copy = pltpu.make_async_copy(q_new, q_out, side_sem.at[1])
    p_copy.start()
    q_copy.start()
    hi, mid, _ = split3(q_new[...].T)
    q_split = jnp.concatenate([hi, mid, hi], axis=1)

    def store(i):
        at = pl.ds(i * STRIDE, STRIDE)
        return pltpu.make_async_copy(stage.at[:, at], new_errors.at[:, at], out_sem.at[i])

    for i in range(ROWS // STRIDE):
        at = pl.ds(i * STRIDE, STRIDE)
        delta = jnp.dot(q_split, p_split[:, at], preferred_element_type=F32)
        stage[:, at] = (merged[:, at].astype(F32) - delta).astype(BF16)
        store(i).start()
    p_copy.wait()
    q_copy.wait()
    for i in range(ROWS // STRIDE):
        store(i).wait()


def body(grads, errors, q_start):
    hbm_spec = pl.BlockSpec(memory_space=pltpu.HBM)
    vmem_spec = pl.BlockSpec(memory_space=pltpu.VMEM)
    dma = pltpu.SemaphoreType.DMA
    tile = (8, 128)
    strip = (8, WIDE)
    merged, p_split, p_hat, q_new = pl.pallas_call(
        kernel,
        name="factors",
        out_shape=(
            jax.ShapeDtypeStruct((COLS, ROWS), BF16),
            jax.ShapeDtypeStruct((3 * RANK, ROWS), BF16),
            jax.ShapeDtypeStruct((RANK, ROWS), F32),
            jax.ShapeDtypeStruct((RANK, COLS), F32),
        ),
        in_specs=[hbm_spec, hbm_spec, hbm_spec],
        out_specs=(vmem_spec,) * 4,
        scratch_shapes=[
            pltpu.VMEM((RANK, COLS), F32),
            pltpu.VMEM((COLS, ROWS), BF16),
            pltpu.VMEM((COLS, ROWS), BF16),
            pltpu.VMEM((3 * RANK, ROWS), BF16),
            pltpu.VMEM((64,) + tile, F32),
            pltpu.VMEM((32,) + tile, F32),
            pltpu.VMEM((32,) + tile, F32),
            pltpu.VMEM((31,) + tile, F32),
            pltpu.VMEM(tile, F32),
            pltpu.VMEM((8,) + tile, F32),
            pltpu.VMEM((64,) + tile, F32),
            pltpu.VMEM((4,) + strip, F32),
            pltpu.VMEM((3,) + strip, F32),
            pltpu.VMEM(strip, F32),
            pltpu.VMEM((8,) + strip, F32),
            pltpu.VMEM((4,) + strip, F32),
            pltpu.VMEM((COLS, ROWS // 2), F32),
            pltpu.VMEM((COLS, ROWS // 2), F32),
            pltpu.VMEM((COLS, ROWS // 2), BF16),
            pltpu.VMEM((COLS, ROWS // 2), BF16),
            pltpu.SemaphoreType.REGULAR,
            dma((STEPS // 2,)),
            dma((STEPS // 2,)),
            dma,
            dma((2, STEPS)),
        ]
        + [dma] * 7
        + [dma((4,))]
        + [dma] * 8,
        compiler_params=pltpu.CompilerParams(
            collective_id=0, has_side_effects=True, vmem_limit_bytes=32 * 1024 * 1024
        ),
    )(*(pltpu.with_memory_space_constraint(a, pltpu.HBM) for a in (grads[0].T, errors[0].T, q_start.T)))
    new_errors, p_hat, q_new = pl.pallas_call(
        update_kernel,
        name="update",
        out_shape=(
            jax.ShapeDtypeStruct((COLS, ROWS), BF16),
            jax.ShapeDtypeStruct((RANK, ROWS), F32),
            jax.ShapeDtypeStruct((RANK, COLS), F32),
        ),
        in_specs=[vmem_spec] * 4,
        out_specs=(hbm_spec,) * 3,
        scratch_shapes=[pltpu.VMEM((COLS, ROWS), BF16), dma((ROWS // STRIDE,)), dma((2,))],
        compiler_params=pltpu.CompilerParams(vmem_limit_bytes=16 * 1024 * 1024),
    )(merged, p_split, p_hat, q_new)
    return new_errors.T[None], p_hat.T, q_new.T


def solution(mesh):
    placed = (P("dp", None, "tensor"), P("dp", None, "tensor"), P("tensor", None))
    return jax.shard_map(
        body,
        mesh=mesh,
        in_specs=placed,
        out_specs=(P("dp", None, "tensor"), P(), P("tensor", None)),
        check_vma=False,
    )
```

```python
import functools

import jax
import jax.numpy as jnp
from jax import lax
from jax.experimental import pallas as pl
from jax.experimental.pallas import tpu as pltpu
from jax.sharding import PartitionSpec as P

MESH = pl.DeviceIdType.MESH
HIGHEST = lax.Precision.HIGHEST
F32, BF16 = jnp.float32, jnp.bfloat16

RANK = 32
ROWS = 2048
COLS = 352
WIDE = 384
STEP = 256
STEPS = ROWS // STEP
STRIDE = 512

FAR = {0: 0, 1: 1, 2: 2, 3: 1}
OFFSETS = sorted(
    ((j, y, x) for j in range(2) for y in range(4) for x in range(4) if (j, y, x) != (0, 0, 0)),
    key=lambda o: -(o[0] + FAR[o[1]] + FAR[o[2]]),
)
GROUPS = [4, 3, 5, 2, 6, 1, 7]


def split3(value):
    hi = value.astype(BF16)
    rest = value - hi.astype(F32)
    mid = rest.astype(BF16)
    lo = (rest - mid.astype(F32)).astype(BF16)
    return hi, mid, lo


def kernel(
    grads, errors, q_start, merged_out, p_split, p_out, q_out,
    q_in, gbuf, ebuf, parts_buf, pt, core_rx, a_src, a_rx, b_src, b_rx, p_full,
    q_part, d_rx, e_src, e_rx, q_full, m_src, m_rx, m_hi, m_lo,
    ready, m_send, m_recv, q_sem, load_sem, core_send, core_recv, a_send, a_recv, b_send, b_recv, c_send, c_recv,
    f_send, f_recv, d_send, d_recv, e_send, e_recv, g_send, g_recv,
):
    dp, tensor = lax.axis_index("dp"), lax.axis_index("tensor")
    z, core = lax.div(dp, 2), lax.rem(dp, 2)
    group, bit = lax.div(z, 2), lax.rem(z, 2)
    member = lax.rem(bit + lax.div(group, 4), 2)
    y, x = lax.div(tensor, 4), lax.rem(tensor, 4)
    columns_of = [lax.rem(x + k, 4) for k in range(4)]
    rows_of = [lax.rem(y + k, 4) * 4 for k in range(4)]
    members = [member, 1 - member]
    in_pair = [dp, 4 * group + 2 * (1 - bit) + core]

    def plane_peer(o):
        t = rows_of[o[1]] + columns_of[o[2]]
        return (in_pair[o[0]], t), members[o[0]] * 16 + t

    def group_at(a):
        return (4 * a + 2 * (member if a < 4 else 1 - member) + core, tensor)

    def group_peer(k):
        a = lax.rem(group + k, 8)
        return (4 * a + 2 * lax.rem(member + lax.div(a, 4), 2) + core, tensor)

    other = 1 - core
    sibling = (dp + other - core, tensor)
    beside = (in_pair[1], tensor)
    across = (in_pair[1] + other - core, tensor)
    mine = member * 16 + tensor

    def cols(i):
        return pl.ds(pl.multiple_of(i * STEP, STEP), STEP)

    def half_at(i):
        return (other if i < STEPS // 2 else core) * (STEPS // 2) + i % (STEPS // 2)

    def load(i):
        at = half_at(i)
        return (
            pltpu.make_async_copy(grads.at[:, cols(at)], gbuf.at[:, cols(at)], load_sem.at[0, i]),
            pltpu.make_async_copy(errors.at[:, cols(at)], ebuf.at[:, cols(at)], load_sem.at[1, i]),
        )

    q_copy = pltpu.make_async_copy(q_start, q_in, q_sem)
    q_copy.start()
    for i in range(2):
        for copy in load(i):
            copy.start()

    barrier = pltpu.get_barrier_semaphore()
    for a in range(8):

        @pl.when(group < a)
        def _():
            pl.semaphore_signal(barrier, inc=1, device_id=group_at(a), device_id_type=MESH)

    for o in OFFSETS:
        pl.semaphore_signal(barrier, inc=1, device_id=plane_peer(o)[0], device_id_type=MESH)
    pl.semaphore_signal(barrier, inc=1, device_id=across, device_id_type=MESH)
    pl.semaphore_signal(barrier, inc=1, device_id=sibling, device_id_type=MESH)

    for i in range(2, STEPS):
        for copy in load(i):
            copy.start()
    q_copy.wait()
    q_narrow = q_in[...].astype(BF16)

    def left(i):
        for copy in load(i):
            copy.wait()
        at = half_at(i)
        merged = (gbuf[:, cols(at)].astype(F32) + ebuf[:, cols(at)].astype(F32)).astype(BF16)
        merged_out[:, cols(at)] = merged
        part = jnp.dot(q_narrow, merged, preferred_element_type=F32)
        for h in range(2):
            pt[pl.ds(at * 8 + h * 4, 4)] = part[:, h * 128 : (h + 1) * 128].reshape(4, 8, 128)

    for i in range(STEPS):
        left(i)
    pl.semaphore_wait(barrier, len(OFFSETS) + 2 + group)
    for a in range(8):

        @pl.when(group > a)
        def _():
            pl.semaphore_signal(ready, inc=1, device_id=group_at(a), device_id_type=MESH)

    core_copies = [
        pltpu.make_async_remote_copy(
            src_ref=pt.at[pl.ds(other * 32 + m * 16, 16)], dst_ref=core_rx.at[pl.ds(m * 16, 16)],
            send_sem=core_send.at[n], recv_sem=core_recv.at[n], device_id=sibling, device_id_type=MESH,
        )
        for n, m in enumerate((members[1], members[0]))
    ]
    for copy in core_copies:
        copy.start()
    for i in range(STEPS // 2):
        m_src[:, i * STEP : (i + 1) * STEP] = merged_out[:, cols(half_at(i))].astype(F32)

    def send(n):
        device, chunk = plane_peer(OFFSETS[n])
        pltpu.make_async_remote_copy(
            src_ref=a_src.at[chunk], dst_ref=a_rx.at[n],
            send_sem=a_send, recv_sem=a_recv, device_id=device, device_id_type=MESH,
        ).start()

    first = [n for n, o in enumerate(OFFSETS) if o[0] == 1 and FAR[o[1]] + FAR[o[2]] >= 3]
    rest = [n for n in range(len(OFFSETS)) if n not in first]
    for copy, m, which in zip(core_copies, (members[1], members[0]), (first, rest)):
        copy.wait_recv()
        part = pl.ds(m * 16, 16)
        a_src[part] = pt[pl.ds(core * 32 + m * 16, 16)] + core_rx[part]
        for n in which:
            send(n)

    def swap(i):
        part = pl.ds(i * STEP, STEP)
        return pltpu.make_async_remote_copy(
            src_ref=m_src.at[:, part], dst_ref=m_rx.at[:, part],
            send_sem=m_send.at[i], recv_sem=m_recv.at[i], device_id=sibling, device_id_type=MESH,
        )

    for i in range(STEPS // 2):
        swap(i).start()

    def all_of(ref, send, recv):
        return pltpu.make_async_remote_copy(
            src_ref=ref, dst_ref=ref, send_sem=send, recv_sem=recv, device_id=sibling, device_id_type=MESH
        )

    all_a = all_of(a_rx, a_send, a_recv)
    all_a.wait_recv()
    total = a_src[mine]
    for n in range(len(OFFSETS)):
        total = total + a_rx[n]
    b_src[...] = total
    b_rx[group] = total

    def spread(a):
        pltpu.make_async_remote_copy(
            src_ref=b_src, dst_ref=b_rx.at[group],
            send_sem=b_send, recv_sem=b_recv, device_id=group_at(a), device_id_type=MESH,
        ).start()

    for a in range(7):

        @pl.when(group > a)
        def _():
            spread(a)

    @pl.when(group < 7)
    def _():
        pl.semaphore_wait(ready, 7 - group)

    for a in range(7, 0, -1):

        @pl.when(group < a)
        def _():
            spread(a)

    for i in range(STEPS // 2):
        part = slice(i * STEP, (i + 1) * STEP)
        swap(i).wait_recv()
        both = merged_out[:, cols(core * (STEPS // 2) + i)].astype(F32) + m_rx[:, part]
        hi = both.astype(BF16)
        m_hi[:, part] = hi
        m_lo[:, part] = (both - hi.astype(F32)).astype(BF16)

    all_b = all_of(b_rx.at[pl.ds(0, 7)], b_send, b_recv)
    all_b.wait_recv()
    total = b_rx[0]
    for k in range(1, 8):
        total = total + b_rx[k]
    p_full[core * 32 + mine] = total
    batch = lax.div(mine, 8)

    for n, o in enumerate(OFFSETS):
        pltpu.make_async_remote_copy(
            src_ref=p_full.at[core * 32 + mine], dst_ref=p_full.at[core * 32 + mine],
            send_sem=c_send, recv_sem=c_recv.at[batch], device_id=plane_peer(o)[0], device_id_type=MESH,
        ).start()
    def left_parts(at):
        tiles = [p_full[pl.ds(at * 8 + h * 4, 4)].reshape(RANK, 128) for h in range(2)]
        parts = jnp.concatenate(split3(jnp.concatenate(tiles, axis=1)), axis=0)
        parts_buf[:, cols(at)] = parts
        return parts

    turned = (((1,), (1,)), ((), ()))
    acc = jnp.zeros((3 * RANK, COLS), F32)
    for i in range(STEPS // 2):
        this = lax.rem(member * 2 + i, 4)

        @pl.when(batch == this)
        def _():
            all_of(p_full.at[pl.ds(0, 7)], c_send, c_recv.at[this]).wait_recv()

        @pl.when(batch != this)
        def _():
            all_of(p_full.at[pl.ds(0, 8)], c_send, c_recv.at[this]).wait_recv()

        parts = left_parts(core * (STEPS // 2) + this)
        acc = acc + lax.dot_general(parts, m_lo[:, cols(this)], turned, preferred_element_type=F32)
        acc = acc + lax.dot_general(parts, m_hi[:, cols(this)], turned, preferred_element_type=F32)
    half = pl.ds(core * 32, 32)
    half_copy = pltpu.make_async_remote_copy(
        src_ref=p_full.at[half], dst_ref=p_full.at[half],
        send_sem=f_send, recv_sem=f_recv, device_id=sibling, device_id_type=MESH,
    )
    half_copy.start()
    acc = acc[2 * RANK :] + acc[RANK : 2 * RANK] + acc[0:RANK]
    q_part[:, :, 0:COLS] = acc.reshape(4, 8, COLS)
    q_part[:, :, COLS:] = jnp.zeros((4, 8, WIDE - COLS), F32)

    def owner(j, c):
        return j * 2 + c

    me = owner(member, core)
    partners = (
        (across, owner(1 - member, other)),
        (beside, owner(1 - member, core)),
        (sibling, owner(member, other)),
    )
    for n, (device, chunk) in enumerate(partners):
        pltpu.make_async_remote_copy(
            src_ref=q_part.at[chunk], dst_ref=d_rx.at[n],
            send_sem=d_send, recv_sem=d_recv, device_id=device, device_id_type=MESH,
        ).start()
    all_d = all_of(d_rx, d_send, d_recv)
    all_d.wait_recv()
    total = q_part[me] + d_rx[0] + d_rx[1] + d_rx[2]
    e_src[...] = total
    e_rx[group] = total
    for k in GROUPS:
        pltpu.make_async_remote_copy(
            src_ref=e_src, dst_ref=e_rx.at[group],
            send_sem=e_send, recv_sem=e_recv, device_id=group_peer(k), device_id_type=MESH,
        ).start()

    half_copy.wait_recv()
    for i in range(STEPS // 2):
        left_parts(other * (STEPS // 2) + i)
    gram = lax.dot_general(
        parts_buf[...], parts_buf[...], (((1,), (1,)), ((), ())), preferred_element_type=F32
    )
    gram = gram[2 * RANK :] + gram[RANK : 2 * RANK] + gram[0:RANK]
    gram = gram[:, 2 * RANK :] + gram[:, RANK : 2 * RANK] + gram[:, 0:RANK]

    row = lax.broadcasted_iota(jnp.int32, (RANK, 2 * RANK), 0)
    col = lax.broadcasted_iota(jnp.int32, (RANK, 2 * RANK), 1)
    unit = jnp.where(col == row + RANK, 1.0, 0.0).astype(F32)
    work = jnp.concatenate([gram, unit[:, RANK:]], axis=1)
    below = lax.broadcasted_iota(jnp.int32, (RANK, 1), 0)
    for k in range(RANK - 1):
        pivot = work[k : k + 1, :]
        factor = work[:, k : k + 1] / work[k : k + 1, k : k + 1]
        work = work - jnp.where(below > k, factor, 0.0) * pivot
    diagonal = jnp.sum(jnp.where(row == col, work, 0.0), axis=1, keepdims=True)
    inverse = work[:, RANK:] / jnp.sqrt(diagonal)

    for i in range(STEPS):
        tiles = [p_full[pl.ds(i * 8 + h * 4, 4)].reshape(RANK, 128) for h in range(2)]
        p_hat = jnp.dot(inverse, jnp.concatenate(tiles, axis=1), precision=HIGHEST, preferred_element_type=F32)
        p_out[:, cols(i)] = p_hat
        hi, mid, _ = split3(p_hat)
        p_split[:, cols(i)] = jnp.concatenate([hi, hi, mid], axis=0)

    hi, mid, lo = split3(inverse)
    inverse_split = jnp.concatenate([hi, hi, mid, mid, hi, lo], axis=1)

    all_e = all_of(e_rx.at[pl.ds(0, 7)], e_send, e_recv)
    all_e.wait_recv()
    total = e_rx[0]
    for k in range(1, 8):
        total = total + e_rx[k]
    q_full[me] = total
    for n, (device, _) in enumerate(partners):
        pltpu.make_async_remote_copy(
            src_ref=q_full.at[me], dst_ref=q_full.at[me],
            send_sem=g_send, recv_sem=g_recv, device_id=device, device_id_type=MESH,
        ).start()
    all_g = all_of(q_full.at[pl.ds(0, 3)], g_send, g_recv)
    all_g.wait_recv()
    q_sum = q_full[...].reshape(RANK, WIDE)
    hi, mid, lo = split3(q_sum)
    q_stack = jnp.concatenate([hi, mid, hi, mid, lo, hi], axis=0)
    q_new = jnp.dot(inverse_split, q_stack, preferred_element_type=F32) * (1.0 / 32.0)
    q_out[...] = q_new[:, 0:COLS]
    for copy in core_copies:
        copy.wait_send()
    all_a.wait_send()
    all_b.wait_send()
    all_of(p_full.at[pl.ds(0, 31)], c_send, c_recv.at[0]).wait_send()
    half_copy.wait_send()
    for i in range(STEPS // 2):
        swap(i).wait_send()
    all_d.wait_send()
    all_e.wait_send()
    all_g.wait_send()


def update_kernel(merged, p_split, p_hat, q_new, new_errors, p_out, q_out, stage, out_sem, side_sem):
    p_copy = pltpu.make_async_copy(p_hat, p_out, side_sem.at[0])
    q_copy = pltpu.make_async_copy(q_new, q_out, side_sem.at[1])
    p_copy.start()
    q_copy.start()
    hi, mid, _ = split3(q_new[...].T)
    q_split = jnp.concatenate([hi, mid, hi], axis=1)

    def store(i):
        at = pl.ds(i * STRIDE, STRIDE)
        return pltpu.make_async_copy(stage.at[:, at], new_errors.at[:, at], out_sem.at[i])

    for i in range(ROWS // STRIDE):
        at = pl.ds(i * STRIDE, STRIDE)
        delta = jnp.dot(q_split, p_split[:, at], preferred_element_type=F32)
        stage[:, at] = (merged[:, at].astype(F32) - delta).astype(BF16)
        store(i).start()
    p_copy.wait()
    q_copy.wait()
    for i in range(ROWS // STRIDE):
        store(i).wait()


def body(grads, errors, q_start):
    hbm_spec = pl.BlockSpec(memory_space=pltpu.HBM)
    vmem_spec = pl.BlockSpec(memory_space=pltpu.VMEM)
    dma = pltpu.SemaphoreType.DMA
    tile = (8, 128)
    strip = (8, WIDE)
    merged, p_split, p_hat, q_new = pl.pallas_call(
        kernel,
        name="factors",
        out_shape=(
            jax.ShapeDtypeStruct((COLS, ROWS), BF16),
            jax.ShapeDtypeStruct((3 * RANK, ROWS), BF16),
            jax.ShapeDtypeStruct((RANK, ROWS), F32),
            jax.ShapeDtypeStruct((RANK, COLS), F32),
        ),
        in_specs=[hbm_spec, hbm_spec, hbm_spec],
        out_specs=(vmem_spec,) * 4,
        scratch_shapes=[
            pltpu.VMEM((RANK, COLS), F32),
            pltpu.VMEM((COLS, ROWS), BF16),
            pltpu.VMEM((COLS, ROWS), BF16),
            pltpu.VMEM((3 * RANK, ROWS), BF16),
            pltpu.VMEM((64,) + tile, F32),
            pltpu.VMEM((32,) + tile, F32),
            pltpu.VMEM((32,) + tile, F32),
            pltpu.VMEM((31,) + tile, F32),
            pltpu.VMEM(tile, F32),
            pltpu.VMEM((8,) + tile, F32),
            pltpu.VMEM((64,) + tile, F32),
            pltpu.VMEM((4,) + strip, F32),
            pltpu.VMEM((3,) + strip, F32),
            pltpu.VMEM(strip, F32),
            pltpu.VMEM((8,) + strip, F32),
            pltpu.VMEM((4,) + strip, F32),
            pltpu.VMEM((COLS, ROWS // 2), F32),
            pltpu.VMEM((COLS, ROWS // 2), F32),
            pltpu.VMEM((COLS, ROWS // 2), BF16),
            pltpu.VMEM((COLS, ROWS // 2), BF16),
            pltpu.SemaphoreType.REGULAR,
            dma((STEPS // 2,)),
            dma((STEPS // 2,)),
            dma,
            dma((2, STEPS)),
        ]
        + [dma((2,))] * 2
        + [dma] * 5
        + [dma((4,))]
        + [dma] * 8,
        compiler_params=pltpu.CompilerParams(
            collective_id=0, has_side_effects=True, vmem_limit_bytes=32 * 1024 * 1024
        ),
    )(*(pltpu.with_memory_space_constraint(a, pltpu.HBM) for a in (grads[0].T, errors[0].T, q_start.T)))
    new_errors, p_hat, q_new = pl.pallas_call(
        update_kernel,
        name="update",
        out_shape=(
            jax.ShapeDtypeStruct((COLS, ROWS), BF16),
            jax.ShapeDtypeStruct((RANK, ROWS), F32),
            jax.ShapeDtypeStruct((RANK, COLS), F32),
        ),
        in_specs=[vmem_spec] * 4,
        out_specs=(hbm_spec,) * 3,
        scratch_shapes=[pltpu.VMEM((COLS, ROWS), BF16), dma((ROWS // STRIDE,)), dma((2,))],
        compiler_params=pltpu.CompilerParams(vmem_limit_bytes=16 * 1024 * 1024),
    )(merged, p_split, p_hat, q_new)
    return new_errors.T[None], p_hat.T, q_new.T


def solution(mesh):
    placed = (P("dp", None, "tensor"), P("dp", None, "tensor"), P("tensor", None))
    return jax.shard_map(
        body,
        mesh=mesh,
        in_specs=placed,
        out_specs=(P("dp", None, "tensor"), P(), P("tensor", None)),
        check_vma=False,
    )
```
